32 devices in a mesh: rep: 2 (over y), enc: 4 (over z), ans: 2 (over x), sub: 2 (over core).
Axes of the slice: x: 2, y: 2, z: 4, core: 2. Of those that a mesh axis runs over, the one named last changes fastest.
Arguments:
- queries: bfloat16 [4, 4, 256, 4096], P(('rep', 'ans'), 'enc', None, 'sub'), parts along dimension 0, may hold values from -10 to 10
- own_keys: bfloat16 [4, 4, 256, 1024], P(('rep', 'ans'), 'enc', None, 'sub'), parts along dimension 0, may hold values from -6 to 6
- own_values: bfloat16 [4, 4, 256, 1024], P(('rep', 'ans'), 'enc', None, 'sub'), parts along dimension 0, may hold values from -6 to 6
- grad_out: bfloat16 [4, 4, 256, 4096], P(('rep', 'ans'), 'enc', None, 'sub'), parts along dimension 0, may hold values from -6 to 6
- passage_keys: bfloat16 [4, 32, 24, 1024], P(('rep', 'ans'), 'enc', None, 'sub'), parts along dimension 0, may hold values from -10 to 10
- passage_values: bfloat16 [4, 32, 24, 1024], P(('rep', 'ans'), 'enc', None, 'sub'), parts along dimension 0, may hold values from -6 to 6
- citations: int32 [4, 4, 6], P(('rep', 'ans'), 'enc'), parts along dimension 0, may hold values from 0 to 31, as said below
- lengths: int32 [4, 4], P(('rep', 'ans'), 'enc'), parts along dimension 0, may hold values from 64 to 256
Outputs:
- grad_queries: bfloat16 [4, 4, 256, 4096], P(('rep', 'ans'), 'enc', None, 'sub'), parts along dimension 0
- grad_own_keys: bfloat16 [4, 4, 256, 1024], P(('rep', 'ans'), 'enc', None, 'sub'), parts along dimension 0
- grad_own_values: bfloat16 [4, 4, 256, 1024], P(('rep', 'ans'), 'enc', None, 'sub'), parts along dimension 0
- grad_passage_keys: bfloat16 [4, 32, 24, 1024], P(('rep', 'ans'), 'enc', None, 'sub'), parts along dimension 0
- grad_passage_values: bfloat16 [4, 32, 24, 1024], P(('rep', 'ans'), 'enc', None, 'sub'), parts along dimension 0
The draws below stay inside these ranges and needn't reach their ends.
There are 2 independent parts, one for each index of `rep`. The reference program is written for one: setup_inputs(seed, part) draws one part's arguments, and reference() takes and returns one part's arrays. A program takes and returns all parts, laid end to end along the dimension named above; each array names one. Nothing has to cross between parts.
Inputs may be any that keep to these rules, and one draw needn't show every extreme that they name: `citations`: each request cites 6 different passages of its own group. Passage p is held by index p // 8 of enc. The requests of one index of enc cite together at most 2 different passages of any one holder, and one request of each index of enc cites 2 passages of one holder.
All inputs are finite; a program needn't handle non-finite values.
Results may differ from the reference program's by a relative error of at most 0.012.
The reference program's roundings to bfloat16 on the way count: a program that leaves them out, or rounds other values in their place, can miss the bound.
Values may be sent and summed in bfloat16 or wider, within the bound.
A program may use at most 64 MiB of HBM per device.

```python
import math
import jax
import jax.numpy as jnp
from jax import lax

HEADS = 32
KV_HEADS = 8
HEAD_DIM = 128
QLEN = 256
PLEN = 24
CAP = 2
P_DEV = 8
REQ_DEV = 1
GROUPS = 2
PASSAGES = 32
REQS = 4
CITE = 6
N_ENC = 4


def draw_queries(key, part):
    key = jax.random.fold_in(key, 5)
    draw_dims = (GROUPS, REQS, QLEN, HEADS * HEAD_DIM)
    return jnp.clip(jax.random.normal(key, draw_dims, jnp.float32), -4.0, 4.0).astype(jnp.bfloat16)


def draw_passage_keys(key, part):
    key = jax.random.fold_in(key, 6)
    draw_dims = (GROUPS, PASSAGES, PLEN, KV_HEADS * HEAD_DIM)
    return jnp.clip(jax.random.normal(key, draw_dims, jnp.float32), -4.0, 4.0).astype(jnp.bfloat16)


def draw_lengths(key, part):
    key = jax.random.fold_in(key, 7)
    lowest = max(2, QLEN // 4)
    drawn_lengths = jax.random.randint(key, (GROUPS, REQS), lowest, QLEN + 1)
    return drawn_lengths.at[0, 0].set(QLEN).astype(jnp.int32)


def draw_citations(key, part):
    key = jax.random.fold_in(key, 11)
    first_key, second_key, third_key = jax.random.split(key, 3)
    device_count = GROUPS * N_ENC
    slot_count = N_ENC * CAP
    pool_keys = jax.random.split(first_key, device_count * N_ENC)
    pool_rows = jax.vmap(lambda single_key: jax.random.permutation(single_key, P_DEV)[:CAP])(pool_keys)
    pool_rows = pool_rows.reshape(device_count, slot_count)
    slot_owner = jnp.arange(slot_count, dtype=jnp.int32) // CAP
    pool_ids = slot_owner[None, :] * P_DEV + pool_rows
    request_total = device_count * REQ_DEV
    request_keys = jax.random.split(second_key, request_total)
    forced_owner = jax.random.randint(third_key, (request_total,), 0, N_ENC)

    def pick_slots(single_key, owner_value):
        ranking = jax.random.permutation(single_key, slot_count) + CAP
        slot_index = jnp.arange(slot_count, dtype=jnp.int32)
        ranking = jnp.where(slot_index // CAP == owner_value, slot_index % CAP, ranking)
        return jnp.argsort(ranking, stable=True)[:CITE]
    picked = jax.vmap(pick_slots)(request_keys, forced_owner).reshape(device_count, REQ_DEV, CITE)
    widened = jnp.broadcast_to(pool_ids[:, None, :], (device_count, REQ_DEV, slot_count))
    cited_ids = jnp.take_along_axis(widened, picked, axis=2)
    return cited_ids.reshape(GROUPS, REQS, CITE).astype(jnp.int32)


def block_levels(rng, shape, pieces, low, high):
    def one(position, blocks):
        heights = jax.random.uniform(jax.random.fold_in(jax.random.fold_in(rng, 6), position), (blocks,), jnp.float32, low / len(pieces), high / len(pieces))
        return jnp.repeat(jnp.exp(heights), shape[position] // blocks).reshape((-1,) + (1,) * (len(shape) - position - 1))

    gain = one(*pieces[0])
    for cut in pieces[1:]:
        gain = gain * one(*cut)
    return gain


def normal_values(rng, extent, deviation, limit, cuts=(), kind=jnp.bfloat16):
    array = jax.random.normal(rng, extent, jnp.float32) * deviation
    if len(cuts) > 0:
        array = block_levels(rng, extent, cuts, -0.22, 0.18) * array
    return jnp.clip(array, min=-limit, max=limit).astype(kind)


def setup_inputs(seed: int = 0, part: int = 0) -> dict:
    streams_of = jax.random.split(jax.random.key(seed), 9)
    part_keys = jax.random.split(jax.random.fold_in(streams_of[8], part), 9)
    queries = draw_queries(jax.random.fold_in(jax.random.fold_in(streams_of[8], part), 71), part)
    own_keys = normal_values(part_keys[1], (GROUPS, REQS, QLEN, KV_HEADS * HEAD_DIM), 1.0, 6.0, ((0, 2), (1, 4), (3, 2)))
    own_values = normal_values(part_keys[2], (GROUPS, REQS, QLEN, KV_HEADS * HEAD_DIM), 1.0, 6.0, ((0, 2), (1, 4), (3, 2)))
    grad_out = normal_values(part_keys[3], (GROUPS, REQS, QLEN, HEADS * HEAD_DIM), 1.0, 6.0, ((0, 2), (1, 4), (3, 2)))
    passage_keys = draw_passage_keys(jax.random.fold_in(jax.random.fold_in(streams_of[8], part), 71), part)
    passage_values = normal_values(part_keys[5], (GROUPS, PASSAGES, PLEN, KV_HEADS * HEAD_DIM), 1.0, 6.0, ((0, 2), (1, 4), (3, 2)))
    citations = draw_citations(jax.random.fold_in(jax.random.fold_in(streams_of[8], part), 71), part)
    lengths = draw_lengths(jax.random.fold_in(jax.random.fold_in(streams_of[8], part), 71), part)
    return {"queries": queries, "own_keys": own_keys, "own_values": own_values, "grad_out": grad_out, "passage_keys": passage_keys, "passage_values": passage_values, "citations": citations, "lengths": lengths}


THETA = 500000.0

def rotate(values, positions, direction):
    dims_shape = values.shape
    head_count = dims_shape[-1] // HEAD_DIM
    half_dim = HEAD_DIM // 2
    split_parts = values.reshape(dims_shape[:-1] + (head_count, 2, half_dim))
    inv_freq = THETA ** (-2.0 * jnp.arange(half_dim, dtype=jnp.float32) / HEAD_DIM)
    angles = positions.astype(jnp.float32)[:, None] * inv_freq[None, :]
    cosine = jnp.cos(angles)[:, None, :]
    sine_part = direction * jnp.sin(angles)[:, None, :]
    first_half = split_parts[..., 0, :]
    second_half = split_parts[..., 1, :]
    turned = jnp.stack([first_half * cosine - second_half * sine_part, second_half * cosine + first_half * sine_part], axis=-2)
    return turned.reshape(dims_shape)

def product(form, left, right):
    return jnp.einsum(form, left.astype(jnp.float32), right.astype(jnp.float32))

def backward_one(query_rows, own_key_rows, own_value_rows, grad_rows, cited_keys, cited_values, length_value):
    query_count, feature_count = query_rows.shape
    cite_count, passage_len, key_features = cited_keys.shape
    kv_count = key_features // HEAD_DIM
    group_size = feature_count // key_features
    prefix = cite_count * passage_len
    key_count = prefix + query_count
    query_pos = prefix + jnp.arange(query_count, dtype=jnp.int32)
    key_pos = jnp.arange(key_count, dtype=jnp.int32)
    rot_queries = rotate(query_rows.astype(jnp.float32), query_pos, 1.0).astype(jnp.bfloat16)
    all_keys = jnp.concatenate([cited_keys.reshape(prefix, key_features), own_key_rows], axis=0)
    rot_keys = rotate(all_keys.astype(jnp.float32), key_pos, 1.0).astype(jnp.bfloat16)
    all_values = jnp.concatenate([cited_values.reshape(prefix, key_features), own_value_rows], axis=0)
    live_rows = jnp.arange(query_count, dtype=jnp.int32) < length_value
    live_grad = jnp.where(live_rows[:, None], grad_rows, jnp.zeros_like(grad_rows))
    query_four = rot_queries.reshape(query_count, kv_count, group_size, HEAD_DIM)
    grad_four = live_grad.reshape(query_count, kv_count, group_size, HEAD_DIM)
    key_three = rot_keys.reshape(key_count, kv_count, HEAD_DIM)
    value_three = all_values.reshape(key_count, kv_count, HEAD_DIM)
    score_scale = 1.0 / math.sqrt(HEAD_DIM)
    scores = product('qcgd,kcd->cgqk', query_four, key_three) * score_scale
    allowed = (key_pos[None, :] < prefix) | (key_pos[None, :] - prefix <= jnp.arange(query_count, dtype=jnp.int32)[:, None])
    scores = jnp.where(allowed, scores, -1e+30)
    highest = lax.optimization_barrier(jnp.max(scores, axis=-1, keepdims=True))
    weights = jnp.exp(scores - highest)
    weights = weights / lax.optimization_barrier(jnp.sum(weights, axis=-1, keepdims=True))
    weights_low = weights.astype(jnp.bfloat16)
    grad_values = product('cgqk,qcgd->kcd', weights_low, grad_four).reshape(key_count, key_features)
    grad_weights = product('qcgd,kcd->cgqk', grad_four, value_three)
    center = lax.optimization_barrier(jnp.sum(grad_weights * weights, axis=-1, keepdims=True))
    grad_scores = (weights * (grad_weights - center) * score_scale).astype(jnp.bfloat16)
    grad_rot_queries = product('cgqk,kcd->qcgd', grad_scores, key_three).reshape(query_count, feature_count)
    grad_rot_keys = product('cgqk,qcgd->kcd', grad_scores, query_four).reshape(key_count, key_features)
    query_grads = rotate(grad_rot_queries, query_pos, -1.0).astype(jnp.bfloat16)
    key_grads = rotate(grad_rot_keys, key_pos, -1.0)
    value_low = grad_values.astype(jnp.bfloat16)
    key_low = key_grads.astype(jnp.bfloat16)
    return (query_grads, key_low[prefix:], value_low[prefix:], key_low[:prefix].reshape(cite_count, passage_len, key_features), value_low[:prefix].reshape(cite_count, passage_len, key_features))

def reference(queries, own_keys, own_values, grad_out, passage_keys, passage_values, citations, lengths):

    def one_group(group_item):
        group_queries, group_own_keys, group_own_values, group_grads, group_pkeys, group_pvalues, group_cites, group_lengths = group_item
        zeros_acc = jnp.zeros(group_pkeys.shape, jnp.float32)

        def one_request(scan_state, request_item):
            acc_keys, acc_values = scan_state
            query_rows, key_rows, value_rows, grad_rows, cite_row, length_value = request_item
            results = backward_one(query_rows, key_rows, value_rows, grad_rows, group_pkeys[cite_row], group_pvalues[cite_row], length_value)
            acc_keys = acc_keys.at[cite_row].add(results[3].astype(jnp.float32))
            acc_values = acc_values.at[cite_row].add(results[4].astype(jnp.float32))
            return ((acc_keys, acc_values), (results[0], results[1], results[2]))
        final_state, stacked = lax.scan(one_request, (zeros_acc, zeros_acc), (group_queries, group_own_keys, group_own_values, group_grads, group_cites, group_lengths))
        return (stacked[0], stacked[1], stacked[2], final_state[0].astype(jnp.bfloat16), final_state[1].astype(jnp.bfloat16))
    grad_queries, grad_own_keys, grad_own_values, grad_passage_keys, grad_passage_values = lax.map(one_group, (queries, own_keys, own_values, grad_out, passage_keys, passage_values, citations, lengths))
    return (grad_queries, grad_own_keys, grad_own_values, grad_passage_keys, grad_passage_values)
```

```python
import functools
import math

import jax
import jax.numpy as jnp
import numpy as np
from jax import lax
from jax.experimental import pallas as pl
from jax.experimental.pallas import tpu as pltpu
from jax.sharding import PartitionSpec as P

D = 128
CAP = 2
THETA = 500000.0
SCALE = 1.0 / math.sqrt(D)
MESH = pl.DeviceIdType.MESH
F32 = jnp.float32
BF16 = jnp.bfloat16


def tables(count):
    half = D // 2
    inv = np.float32(THETA) ** (np.float32(-2.0) * np.arange(half, dtype=np.float32) / np.float32(D))
    angles = np.arange(count, dtype=np.float32)[:, None] * inv.astype(np.float32)[None, :]
    cos, sin = np.cos(angles), np.sin(angles)
    return np.concatenate([cos, cos, -sin, sin], axis=1).astype(np.float32)


def turn(x, table, sign):
    cos, sin = table[:, :D], table[:, D:]
    return x * cos + sign * (pltpu.roll(x, D // 2, 1) * sin)


def dot_nt(a, b):
    return lax.dot_general(a, b, (((1,), (1,)), ((), ())), preferred_element_type=F32)


def dot_nn(a, b):
    return lax.dot_general(a, b, (((1,), (0,)), ((), ())), preferred_element_type=F32)


def dot_tn(a, b):
    return lax.dot_general(a, b, (((0,), (0,)), ((), ())), preferred_element_type=F32)


def kernel(
    n, cites, lens, q_hbm, ok_hbm, ov_hbm, go_hbm, pk_hbm, pv_hbm, tab_hbm,
    gq, gok, gov, gpk, gpv,
    q, ok, ov, go, pk, pv, tab,
    tile, tiles_in, sendbuf, fwd_in, backbuf, back_in,
    stage, gstage, qr, gl, ko, kp, dsp, es, dps, stats, wrow, slot_of, cite_of,
    load_sem, cs_sem, cr_sem, fs_sem, fr_sem, bs_sem, br_sem,
):
    rows = q.shape[0]
    heads = ok.shape[1] // D
    group = q.shape[1] // ok.shape[1]
    held, plen = pk.shape[0], pk.shape[1]
    ncite = cites.shape[2]
    prefix = ncite * plen
    me = lax.axis_index("enc")

    loads = [
        pltpu.make_async_copy(src, dst, load_sem.at[i])
        for i, (src, dst) in enumerate(
            [
                (pk_hbm.at[0], pk), (pv_hbm.at[0], pv), (tab_hbm, tab),
                (ok_hbm.at[0, 0], ok), (ov_hbm.at[0, 0], ov),
                (q_hbm.at[0, 0], q), (go_hbm.at[0, 0], go),
            ]
        )
    ]
    barrier = pltpu.get_barrier_semaphore()

    @pl.loop(1, n)
    def _(k):
        pl.semaphore_signal(
            barrier, inc=1, device_id={"enc": lax.rem(me + k, n)}, device_id_type=MESH
        )

    for load in loads:
        load.start()

    lane = lax.broadcasted_iota(jnp.int32, (8, D), 1)
    wanted = jnp.full((8, D), -1, jnp.int32)
    for j in range(ncite):
        wanted = jnp.where(lane == j, cites[0, 0, j], wanted)
    tile[...] = wanted
    tiles_in[0] = wanted
    pl.semaphore_wait(barrier, n - 1)

    def ask(k):
        return pltpu.make_async_remote_copy(
            src_ref=tile, dst_ref=tiles_in.at[k],
            send_sem=cs_sem.at[k], recv_sem=cr_sem.at[k],
            device_id={"enc": lax.rem(me + k, n)}, device_id_type=MESH,
        )

    def forward(k, h):
        return pltpu.make_async_remote_copy(
            src_ref=sendbuf.at[k, h], dst_ref=fwd_in.at[k, h],
            send_sem=fs_sem.at[k, h], recv_sem=fr_sem.at[k, h],
            device_id={"enc": lax.rem(me - k + n, n)}, device_id_type=MESH,
        )

    def back(k, h):
        return pltpu.make_async_remote_copy(
            src_ref=backbuf.at[k, h], dst_ref=back_in.at[k, h],
            send_sem=bs_sem.at[k, h], recv_sem=br_sem.at[k, h],
            device_id={"enc": lax.rem(me + k, n)}, device_id_type=MESH,
        )

    @pl.loop(1, n)
    def _(k):
        ask(k).start()

    @pl.loop(0, ncite)
    def _(j):
        mine = cites[0, 0, j]
        owner = lax.div(mine, held)

        def count(i, total):
            other = cites[0, 0, i]
            return total + jnp.where((lax.div(other, held) == owner) & (other < mine), 1, 0)

        rank = lax.fori_loop(0, ncite, count, jnp.int32(0))
        slot_of[j] = lax.rem(owner - me + n, n) * CAP + rank

    @pl.loop(0, n * CAP)
    def _(s):
        def find(j, found):
            return jnp.where(slot_of[j] == s, j, found)

        cite_of[s] = lax.fori_loop(0, ncite, find, jnp.int32(ncite))

    loads[0].wait()
    loads[1].wait()

    def pick(k, target):
        own = tiles_in[k] - me * held
        inside = (own >= 0) & (own < held) & (lane < ncite)
        low = jnp.min(jnp.where(inside, own, held))
        high = jnp.max(jnp.where(inside, own, -1))
        wrow[k, 0] = low
        wrow[k, 1] = jnp.where(high > low, high, held)
        a = jnp.clip(low, 0, held - 1)
        b = jnp.clip(high, 0, held - 1)
        block = jnp.concatenate(
            [pk[a].astype(F32), pk[b].astype(F32), pv[a].astype(F32), pv[b].astype(F32)], axis=0
        ).astype(BF16)
        for h in range(heads):
            target[k, h] = block[:, h * D : (h + 1) * D]

    @pl.loop(1, n)
    def _(k):
        ask(k).wait_recv()
        pick(k, sendbuf)

    @pl.loop(0, heads)
    def _(h):
        @pl.loop(1, n)
        def _(k):
            forward(k, h).start()

    pick(0, fwd_in)
    for load in loads[2:]:
        load.wait()

    limit = lens[0, 0]
    live = lax.broadcasted_iota(jnp.int32, (rows, D), 0) < limit
    causal = lax.broadcasted_iota(jnp.int32, (rows, rows), 0) <= lax.broadcasted_iota(
        jnp.int32, (rows, rows), 1
    )

    @pl.loop(0, heads)
    def _(h):
        own_table = tab[prefix:, :]
        kcols = pl.ds(pl.multiple_of(h * D, D), D)
        key_own = turn(ok[:, kcols].astype(F32), own_table, 1.0).astype(BF16)
        ko[h] = key_own
        value_own = ov[:, kcols]
        for j in range(group):
            cols = pl.ds(pl.multiple_of((h * group + j) * D, D), D)
            query = turn(q[:, cols].astype(F32), own_table, 1.0).astype(BF16)
            grad = jnp.where(live, go[:, cols].astype(F32), 0.0).astype(BF16)
            qr[h, j] = query
            gl[h, j] = grad
            scores = jnp.where(causal, dot_nt(key_own, query) * SCALE, -1e30)
            top = jnp.max(scores, axis=0, keepdims=True)
            weights = jnp.exp(scores - top)
            gw = dot_nt(value_own, grad)
            es[h, j] = weights
            dps[h, j] = gw
            stats[h, j, 0:1, :] = top
            stats[h, j, 1:2, :] = jnp.sum(weights, axis=0, keepdims=True)
            stats[h, j, 2:3, :] = jnp.sum(weights * gw, axis=0, keepdims=True)

    gstage[ncite] = jnp.zeros(gstage.shape[1:], F32)

    @pl.loop(0, heads)
    def _(h):
        @pl.loop(1, n)
        def _(k):
            forward(k, h).wait_recv()

        @pl.loop(0, n)
        def _(k):
            block = fwd_in[k, h].astype(F32)
            for r in range(CAP):
                stage[k * CAP + r, 0] = block[r * plen : (r + 1) * plen]
                stage[k * CAP + r, 1] = block[(CAP + r) * plen : (CAP + r + 1) * plen]

        keys = jnp.concatenate([stage[slot_of[j], 0] for j in range(ncite)], axis=0)
        key_pas = turn(keys, tab[:prefix, :], 1.0).astype(BF16)
        kp[h] = key_pas
        value_pas = jnp.concatenate(
            [stage[slot_of[j], 1] for j in range(ncite)], axis=0
        ).astype(BF16)
        sum_keys = jnp.zeros((prefix, D), F32)
        sum_values = jnp.zeros((prefix, D), F32)
        for j in range(group):
            query, grad = qr[h, j], gl[h, j]
            top = stats[h, j, 0:1, :]
            scores = dot_nt(key_pas, query) * SCALE
            highest = jnp.maximum(top, jnp.max(scores, axis=0, keepdims=True))
            weights = jnp.exp(scores - highest)
            alpha = jnp.exp(top - highest)
            total = stats[h, j, 1:2, :] * alpha + jnp.sum(weights, axis=0, keepdims=True)
            inverse = 1.0 / total
            gw = dot_nt(value_pas, grad)
            center = (
                stats[h, j, 2:3, :] * alpha + jnp.sum(weights * gw, axis=0, keepdims=True)
            ) * inverse
            weights = weights * inverse
            grad_scores = (weights * (gw - center) * SCALE).astype(BF16)
            dsp[h, j] = grad_scores
            sum_values += dot_nn(weights.astype(BF16), grad)
            sum_keys += dot_nn(grad_scores, query)
            stats[h, j, 3:4, :] = alpha * inverse
            stats[h, j, 4:5, :] = center
        sum_keys = turn(sum_keys, tab[:prefix, :], -1.0)
        for j in range(ncite):
            gstage[j, 0] = sum_keys[j * plen : (j + 1) * plen]
            gstage[j, 1] = sum_values[j * plen : (j + 1) * plen]

        def give(k, target):
            a, b = cite_of[k * CAP], cite_of[k * CAP + 1]
            target[k, h] = jnp.concatenate(
                [gstage[a, 0], gstage[b, 0], gstage[a, 1], gstage[b, 1]], axis=0
            ).astype(BF16)

        @pl.loop(1, n)
        def _(k):
            give(k, backbuf)
            back(k, h).start()

        give(0, back_in)

        kcols = pl.ds(pl.multiple_of(h * D, D), D)
        key_own = ko[h]
        own_table = tab[prefix:, :]
        own_keys = jnp.zeros((rows, D), F32)
        own_values = jnp.zeros((rows, D), F32)
        for j in range(group):
            query, grad = qr[h, j], gl[h, j]
            weights = es[h, j] * stats[h, j, 3:4, :]
            grad_scores = (weights * (dps[h, j] - stats[h, j, 4:5, :]) * SCALE).astype(BF16)
            own_values += dot_nn(weights.astype(BF16), grad)
            own_keys += dot_nn(grad_scores, query)
            grad_query = dot_tn(dsp[h, j], key_pas) + dot_tn(grad_scores, key_own)
            cols = pl.ds(pl.multiple_of((h * group + j) * D, D), D)
            gq[0, 0, :, cols] = turn(grad_query, own_table, -1.0).astype(BF16)
        gok[0, 0, :, kcols] = turn(own_keys, own_table, -1.0).astype(BF16)
        gov[0, 0, :, kcols] = own_values.astype(BF16)

    for h in range(heads):
        @pl.loop(1, n)
        def _(k):
            back(k, h).wait_recv()

        @pl.loop(0, held)
        def _(i):
            def add(k, total):
                block = back_in[k, h].astype(F32)
                for r in range(CAP):
                    hit = wrow[k, r] == i
                    total = (
                        total[0] + jnp.where(hit, block[r * plen : (r + 1) * plen], 0.0),
                        total[1]
                        + jnp.where(hit, block[(CAP + r) * plen : (CAP + r + 1) * plen], 0.0),
                    )
                return total

            zero = jnp.zeros((plen, D), F32)
            total = lax.fori_loop(0, n, add, (zero, zero))
            gpk[0, i, :, h * D : (h + 1) * D] = total[0].astype(BF16)
            gpv[0, i, :, h * D : (h + 1) * D] = total[1].astype(BF16)

    @pl.loop(1, n)
    def _(k):
        ask(k).wait_send()

        @pl.loop(0, heads)
        def _(h):
            forward(k, h).wait_send()
            back(k, h).wait_send()


def shards(n, queries, own_keys, own_values, grad_out, pkeys, pvalues, citations, lengths):
    rows, features = queries.shape[2:]
    kfeatures = own_keys.shape[3]
    heads, group = kfeatures // D, features // kfeatures
    held, plen = pkeys.shape[1], pkeys.shape[2]
    ncite = citations.shape[2]
    prefix = ncite * plen
    keys = prefix + rows
    slab = (n, heads, 2 * CAP * plen, D)
    table = jnp.asarray(tables(keys))
    any_spec = pl.BlockSpec(memory_space=pl.ANY)
    smem = pl.BlockSpec(memory_space=pltpu.SMEM)
    vmem = pl.BlockSpec(memory_space=pltpu.VMEM)
    like = lambda x: jax.ShapeDtypeStruct(x.shape, x.dtype)
    flops = 2 * 5 * heads * group * rows * keys * D
    return pl.pallas_call(
        functools.partial(kernel, n),
        out_shape=tuple(like(x) for x in (queries, own_keys, own_values, pkeys, pvalues)),
        in_specs=[smem] * 2 + [any_spec] * 7,
        out_specs=(vmem,) * 5,
        scratch_shapes=[
            pltpu.VMEM((rows, features), BF16),
            pltpu.VMEM((rows, kfeatures), BF16),
            pltpu.VMEM((rows, kfeatures), BF16),
            pltpu.VMEM((rows, features), BF16),
            pltpu.VMEM((held, plen, kfeatures), BF16),
            pltpu.VMEM((held, plen, kfeatures), BF16),
            pltpu.VMEM((keys, 2 * D), F32),
            pltpu.VMEM((8, D), jnp.int32),
            pltpu.VMEM((n, 8, D), jnp.int32),
            pltpu.VMEM(slab, BF16),
            pltpu.VMEM(slab, BF16),
            pltpu.VMEM(slab, BF16),
            pltpu.VMEM(slab, BF16),
            pltpu.VMEM((n * CAP, 2, plen, D), F32),
            pltpu.VMEM((ncite + 1, 2, plen, D), F32),
            pltpu.VMEM((heads, group, rows, D), BF16),
            pltpu.VMEM((heads, group, rows, D), BF16),
            pltpu.VMEM((heads, rows, D), BF16),
            pltpu.VMEM((heads, prefix, D), BF16),
            pltpu.VMEM((heads, group, prefix, rows), BF16),
            pltpu.VMEM((heads, group, rows, rows), F32),
            pltpu.VMEM((heads, group, rows, rows), F32),
            pltpu.VMEM((heads, group, 8, rows), F32),
            pltpu.SMEM((n, CAP), jnp.int32),
            pltpu.SMEM((ncite,), jnp.int32),
            pltpu.SMEM((n * CAP,), jnp.int32),
            pltpu.SemaphoreType.DMA((7,)),
            pltpu.SemaphoreType.DMA((n,)),
            pltpu.SemaphoreType.DMA((n,)),
            pltpu.SemaphoreType.DMA((n, heads)),
            pltpu.SemaphoreType.DMA((n, heads)),
            pltpu.SemaphoreType.DMA((n, heads)),
            pltpu.SemaphoreType.DMA((n, heads)),
        ],
        compiler_params=pltpu.CompilerParams(
            collective_id=0, has_side_effects=True, vmem_limit_bytes=56 * 1024 * 1024
        ),
        cost_estimate=pl.CostEstimate(
            flops=flops, bytes_accessed=6 * 1024 * 1024, transcendentals=heads * group * rows * keys
        ),
    )(citations, lengths, queries, own_keys, own_values, grad_out, pkeys, pvalues, table)


def solution(mesh):
    rows = P(("rep", "ans"), "enc", None, "sub")
    return jax.shard_map(
        functools.partial(shards, mesh.shape["enc"]),
        mesh=mesh,
        in_specs=(rows,) * 6 + (P(("rep", "ans"), "enc", None), P(("rep", "ans"), "enc")),
        out_specs=(rows,) * 5,
        check_vma=False,
    )
```

```python
import functools
import math

import jax
import jax.numpy as jnp
import numpy as np
from jax import lax
from jax.experimental import pallas as pl
from jax.experimental.pallas import tpu as pltpu
from jax.sharding import PartitionSpec as P

D = 128
CAP = 2
THETA = 500000.0
SCALE = 1.0 / math.sqrt(D)
MESH = pl.DeviceIdType.MESH
F32 = jnp.float32
BF16 = jnp.bfloat16


def tables(count):
    half = D // 2
    inv = np.float32(THETA) ** (np.float32(-2.0) * np.arange(half, dtype=np.float32) / np.float32(D))
    angles = np.arange(count, dtype=np.float32)[:, None] * inv.astype(np.float32)[None, :]
    cos, sin = np.cos(angles), np.sin(angles)
    return np.concatenate([cos, cos, -sin, sin], axis=1).astype(np.float32)


def turn(x, table, sign):
    cos, sin = table[:, :D], table[:, D:]
    return x * cos + sign * (pltpu.roll(x, D // 2, 1) * sin)


def dot_nt(a, b):
    return lax.dot_general(a, b, (((1,), (1,)), ((), ())), preferred_element_type=F32)


def dot_nn(a, b):
    return lax.dot_general(a, b, (((1,), (0,)), ((), ())), preferred_element_type=F32)


def dot_tn(a, b):
    return lax.dot_general(a, b, (((0,), (0,)), ((), ())), preferred_element_type=F32)


def kernel(
    n, cites, lens_hbm, q_hbm, ok_hbm, ov_hbm, go_hbm, pk_hbm, pv_hbm, tab_hbm,
    gq, gok, gov, gpk, gpv,
    q, ok, ov, go, pk, pv, tab,
    lens, cites_in, sendbuf, fwd_in, backbuf, back_in,
    stage, gstage, qr, gl, ko, kp, dsp, es, dps, stats, wrow, slot_of, cite_of, place_of, bstage,
    load_sem, cs_sem, cr_sem, fs_sem, fr_sem, bs_sem, br_sem,
):
    rows = q.shape[0]
    heads = ok.shape[1] // D
    group = q.shape[1] // ok.shape[1]
    held, plen = pk.shape[0], pk.shape[1]
    ncite = cites.shape[2]
    prefix = ncite * plen
    me = lax.axis_index("enc")

    loads = [
        pltpu.make_async_copy(src, dst, load_sem.at[i])
        for i, (src, dst) in enumerate(
            [
                (pk_hbm.at[0], pk), (pv_hbm.at[0], pv), (tab_hbm, tab),
                (ok_hbm.at[0, 0], ok), (ov_hbm.at[0, 0], ov),
                (q_hbm.at[0, 0], q), (go_hbm.at[0, 0], go), (lens_hbm, lens),
            ]
        )
    ]
    barrier = pltpu.get_barrier_semaphore()

    @pl.loop(1, n)
    def _(k):
        pl.semaphore_signal(
            barrier, inc=1, device_id={"enc": lax.rem(me + k, n)}, device_id_type=MESH
        )

    for load in loads:
        load.start()

    def ask(k):
        return pltpu.make_async_remote_copy(
            src_ref=cites.at[0], dst_ref=cites_in.at[k],
            send_sem=cs_sem.at[k], recv_sem=cr_sem.at[k],
            device_id={"enc": lax.rem(me + k, n)}, device_id_type=MESH,
        )

    def forward(k, h):
        return pltpu.make_async_remote_copy(
            src_ref=sendbuf.at[k, h], dst_ref=fwd_in.at[k, h],
            send_sem=fs_sem.at[k, h], recv_sem=fr_sem.at[k, h],
            device_id={"enc": lax.rem(me - k + n, n)}, device_id_type=MESH,
        )

    def back(k, h):
        return pltpu.make_async_remote_copy(
            src_ref=backbuf.at[k, h], dst_ref=back_in.at[k, h],
            send_sem=bs_sem.at[k, h], recv_sem=br_sem.at[k, h],
            device_id={"enc": lax.rem(me + k, n)}, device_id_type=MESH,
        )

    def unpack(source, target, h):
        @pl.loop(0, n, unroll=min(n, 4))
        def _(k):
            block = source[k, h].astype(F32)
            for r in range(CAP):
                target[k * CAP + r, 0] = block[r * plen : (r + 1) * plen]
                target[k * CAP + r, 1] = block[(CAP + r) * plen : (CAP + r + 1) * plen]

    def pick(k, target):
        low, high = held, -1
        for j in range(ncite):
            asked = cites[0, 0, j] if isinstance(k, int) else cites_in[k, 0, j]
            own = asked - me * held
            inside = (own >= 0) & (own < held)
            low = jnp.minimum(low, jnp.where(inside, own, held))
            high = jnp.maximum(high, jnp.where(inside, own, -1))
        wrow[k, 0] = low
        wrow[k, 1] = jnp.where(high > low, high, held)
        a = jnp.clip(low, 0, held - 1)
        b = jnp.clip(high, 0, held - 1)
        block = jnp.concatenate(
            [pk[a].astype(F32), pk[b].astype(F32), pv[a].astype(F32), pv[b].astype(F32)], axis=0
        ).astype(BF16)
        for h in range(heads):
            target[k, h] = block[:, h * D : (h + 1) * D]

    @pl.loop(0, ncite)
    def _(j):
        mine = cites[0, 0, j]
        owner = lax.div(mine, held)

        def count(i, total):
            other = cites[0, 0, i]
            return total + jnp.where((lax.div(other, held) == owner) & (other < mine), 1, 0)

        rank = lax.fori_loop(0, ncite, count, jnp.int32(0))
        slot_of[j] = lax.rem(owner - me + n, n) * CAP + rank

    @pl.loop(0, n * CAP)
    def _(s):
        def find(j, found):
            return jnp.where(slot_of[j] == s, j, found)

        cite_of[s] = lax.fori_loop(0, ncite, find, jnp.int32(ncite))

    loads[0].wait()
    loads[1].wait()
    pick(0, fwd_in)
    for load in loads[2:]:
        load.wait()

    limit = lens[0, 0, 0]
    live = lax.broadcasted_iota(jnp.int32, (rows, D), 0) < limit
    causal = lax.broadcasted_iota(jnp.int32, (rows, rows), 0) <= lax.broadcasted_iota(
        jnp.int32, (rows, rows), 1
    )

    def own(h):
        own_table = tab[prefix:, :]
        kcols = pl.ds(pl.multiple_of(h * D, D), D)
        key_own = turn(ok[:, kcols].astype(F32), own_table, 1.0).astype(BF16)
        ko[h] = key_own
        value_own = ov[:, kcols]
        for j in range(group):
            cols = pl.ds(pl.multiple_of((h * group + j) * D, D), D)
            query = turn(q[:, cols].astype(F32), own_table, 1.0).astype(BF16)
            grad = jnp.where(live, go[:, cols].astype(F32), 0.0).astype(BF16)
            qr[h, j] = query
            gl[h, j] = grad
            scores = jnp.where(causal, dot_nt(key_own, query) * SCALE, -1e30)
            top = jnp.max(scores, axis=0, keepdims=True)
            weights = jnp.exp(scores - top)
            gw = dot_nt(value_own, grad)
            es[h, j] = weights
            dps[h, j] = gw
            stats[h, j, 0:1, :] = top
            stats[h, j, 1:2, :] = jnp.sum(weights, axis=0, keepdims=True)
            stats[h, j, 2:3, :] = jnp.sum(weights * gw, axis=0, keepdims=True)

    own(0)
    pl.semaphore_wait(barrier, n - 1)

    @pl.loop(1, n)
    def _(k):
        ask(k).start()


    def serve(k):
        ask(k).wait_recv()
        pick(k, sendbuf)
        for h in range(heads):
            forward(k, h).start()

    @pl.loop(1, n)
    def _(d):
        pl.when(me >= d)(lambda: serve(d))
        pl.when(me + d < n)(lambda: serve(n - d))

    @pl.loop(1, heads)
    def _(h):
        own(h)

    @pl.loop(0, held)
    def _(i):
        @pl.loop(0, n)
        def _(k):
            second = jnp.where(wrow[k, 1] == i, k * CAP + 1, n * CAP)
            place_of[i, k] = jnp.where(wrow[k, 0] == i, k * CAP, second)

    @pl.loop(1, n)
    def _(k):
        ask(k).wait_send()

    gstage[ncite] = jnp.zeros(gstage.shape[1:], F32)

    @pl.loop(0, heads)
    def _(h):
        @pl.loop(1, n)
        def _(k):
            forward(k, h).wait()

        unpack(fwd_in, stage, h)
        keys = jnp.concatenate([stage[slot_of[j], 0] for j in range(ncite)], axis=0)
        key_pas = turn(keys, tab[:prefix, :], 1.0).astype(BF16)
        kp[h] = key_pas
        value_pas = jnp.concatenate(
            [stage[slot_of[j], 1] for j in range(ncite)], axis=0
        ).astype(BF16)
        sum_keys = jnp.zeros((prefix, D), F32)
        sum_values = jnp.zeros((prefix, D), F32)
        for j in range(group):
            query, grad = qr[h, j], gl[h, j]
            top = stats[h, j, 0:1, :]
            scores = dot_nt(key_pas, query) * SCALE
            highest = jnp.maximum(top, jnp.max(scores, axis=0, keepdims=True))
            weights = jnp.exp(scores - highest)
            alpha = jnp.exp(top - highest)
            total = stats[h, j, 1:2, :] * alpha + jnp.sum(weights, axis=0, keepdims=True)
            inverse = 1.0 / total
            gw = dot_nt(value_pas, grad)
            center = (
                stats[h, j, 2:3, :] * alpha + jnp.sum(weights * gw, axis=0, keepdims=True)
            ) * inverse
            weights = weights * inverse
            grad_scores = (weights * (gw - center) * SCALE).astype(BF16)
            dsp[h, j] = grad_scores
            sum_values += dot_nn(weights.astype(BF16), grad)
            sum_keys += dot_nn(grad_scores, query)
            stats[h, j, 3:4, :] = alpha * inverse
            stats[h, j, 4:5, :] = center
        sum_keys = turn(sum_keys, tab[:prefix, :], -1.0)
        for j in range(ncite):
            gstage[j, 0] = sum_keys[j * plen : (j + 1) * plen]
            gstage[j, 1] = sum_values[j * plen : (j + 1) * plen]

        def give(k, target):
            a, b = cite_of[k * CAP], cite_of[k * CAP + 1]
            target[k, h] = jnp.concatenate(
                [gstage[a, 0], gstage[b, 0], gstage[a, 1], gstage[b, 1]], axis=0
            ).astype(BF16)

        @pl.loop(1, n)
        def _(k):
            give(k, backbuf)
            back(k, h).start()

        give(0, back_in)

    @pl.loop(0, heads)
    def _(h):
        key_pas = kp[h]
        kcols = pl.ds(pl.multiple_of(h * D, D), D)
        key_own = ko[h]
        own_table = tab[prefix:, :]
        own_keys = jnp.zeros((rows, D), F32)
        own_values = jnp.zeros((rows, D), F32)
        for j in range(group):
            query, grad = qr[h, j], gl[h, j]
            weights = es[h, j] * stats[h, j, 3:4, :]
            grad_scores = (weights * (dps[h, j] - stats[h, j, 4:5, :]) * SCALE).astype(BF16)
            own_values += dot_nn(weights.astype(BF16), grad)
            own_keys += dot_nn(grad_scores, query)
            grad_query = dot_tn(dsp[h, j], key_pas) + dot_tn(grad_scores, key_own)
            cols = pl.ds(pl.multiple_of((h * group + j) * D, D), D)
            gq[0, 0, :, cols] = turn(grad_query, own_table, -1.0).astype(BF16)
        gok[0, 0, :, kcols] = turn(own_keys, own_table, -1.0).astype(BF16)
        gov[0, 0, :, kcols] = own_values.astype(BF16)

    bstage[n * CAP] = jnp.zeros(bstage.shape[1:], F32)

    @pl.loop(0, heads)
    def _(h):
        @pl.loop(1, n)
        def _(k):
            back(k, h).wait_recv()
            back(k, h).wait_send()

        unpack(back_in, bstage, h)
        kcols = pl.ds(pl.multiple_of(h * D, D), D)
        for i in range(held):
            total = bstage[place_of[i, 0]]
            for k in range(1, n):
                total += bstage[place_of[i, k]]
            gpk[0, i, :, kcols] = total[0].astype(BF16)
            gpv[0, i, :, kcols] = total[1].astype(BF16)


def place(*refs):
    sems = refs[10]
    copies = [pltpu.make_async_copy(refs[i], refs[5 + i], sems.at[i]) for i in range(5)]
    for copy in copies:
        copy.start()
    for copy in copies:
        copy.wait()


def shards(n, queries, own_keys, own_values, grad_out, pkeys, pvalues, citations, lengths):
    rows, features = queries.shape[2:]
    kfeatures = own_keys.shape[3]
    heads, group = kfeatures // D, features // kfeatures
    held, plen = pkeys.shape[1], pkeys.shape[2]
    ncite = citations.shape[2]
    prefix = ncite * plen
    keys = prefix + rows
    slab = (n, heads, 2 * CAP * plen, D)
    table = jnp.asarray(tables(keys))
    hbm = pl.BlockSpec(memory_space=pltpu.HBM)
    smem = pl.BlockSpec(memory_space=pltpu.SMEM)
    vmem = pl.BlockSpec(memory_space=pltpu.VMEM)
    like = lambda x: jax.ShapeDtypeStruct(x.shape, x.dtype)
    flops = 2 * 5 * heads * group * rows * keys * D
    results = pl.pallas_call(
        functools.partial(kernel, n),
        out_shape=tuple(
            pltpu.VMEM(x.shape, x.dtype) for x in (queries, own_keys, own_values, pkeys, pvalues)
        ),
        in_specs=[smem] + [hbm] * 8,
        out_specs=(vmem,) * 5,
        scratch_shapes=[
            pltpu.VMEM((rows, features), BF16),
            pltpu.VMEM((rows, kfeatures), BF16),
            pltpu.VMEM((rows, kfeatures), BF16),
            pltpu.VMEM((rows, features), BF16),
            pltpu.VMEM((held, plen, kfeatures), BF16),
            pltpu.VMEM((held, plen, kfeatures), BF16),
            pltpu.VMEM((keys, 2 * D), F32),
            pltpu.SMEM((1, 1, 1), jnp.int32),
            pltpu.SMEM((n, 1, ncite), jnp.int32),
            pltpu.VMEM(slab, BF16),
            pltpu.VMEM(slab, BF16),
            pltpu.VMEM(slab, BF16),
            pltpu.VMEM(slab, BF16),
            pltpu.VMEM((n * CAP, 2, plen, D), F32),
            pltpu.VMEM((ncite + 1, 2, plen, D), F32),
            pltpu.VMEM((heads, group, rows, D), BF16),
            pltpu.VMEM((heads, group, rows, D), BF16),
            pltpu.VMEM((heads, rows, D), BF16),
            pltpu.VMEM((heads, prefix, D), BF16),
            pltpu.VMEM((heads, group, prefix, rows), BF16),
            pltpu.VMEM((heads, group, rows, rows), F32),
            pltpu.VMEM((heads, group, rows, rows), F32),
            pltpu.VMEM((heads, group, 8, rows), F32),
            pltpu.SMEM((n, CAP), jnp.int32),
            pltpu.SMEM((ncite,), jnp.int32),
            pltpu.SMEM((n * CAP,), jnp.int32),
            pltpu.SMEM((held, n), jnp.int32),
            pltpu.VMEM((n * CAP + 1, 2, plen, D), F32),
            pltpu.SemaphoreType.DMA((8,)),
            pltpu.SemaphoreType.DMA((n,)),
            pltpu.SemaphoreType.DMA((n,)),
            pltpu.SemaphoreType.DMA((n, heads)),
            pltpu.SemaphoreType.DMA((n, heads)),
            pltpu.SemaphoreType.DMA((n, heads)),
            pltpu.SemaphoreType.DMA((n, heads)),
        ],
        compiler_params=pltpu.CompilerParams(
            collective_id=0, has_side_effects=True, vmem_limit_bytes=61 * 1024 * 1024
        ),
        cost_estimate=pl.CostEstimate(
            flops=flops, bytes_accessed=6 * 1024 * 1024, transcendentals=heads * group * rows * keys
        ),
    )(citations, lengths[None], queries, own_keys, own_values, grad_out, pkeys, pvalues, table)
    return pl.pallas_call(
        place,
        out_shape=tuple(like(x) for x in (queries, own_keys, own_values, pkeys, pvalues)),
        in_specs=[pl.BlockSpec(memory_space=pl.ANY)] * 5,
        out_specs=(hbm,) * 5,
        scratch_shapes=[pltpu.SemaphoreType.DMA((5,))],
        compiler_params=pltpu.CompilerParams(vmem_limit_bytes=1024 * 1024),
        cost_estimate=pl.CostEstimate(flops=0, bytes_accessed=2 * 1024 * 1024, transcendentals=0),
    )(*results)


def solution(mesh):
    rows = P(("rep", "ans"), "enc", None, "sub")
    return jax.shard_map(
        functools.partial(shards, mesh.shape["enc"]),
        mesh=mesh,
        in_specs=(rows,) * 6 + (P(("rep", "ans"), "enc", None), P(("rep", "ans"), "enc")),
        out_specs=(rows,) * 5,
        check_vma=False,
    )
```

```python
import functools
import math

import jax
import jax.numpy as jnp
import numpy as np
from jax import lax
from jax.experimental import pallas as pl
from jax.experimental.pallas import tpu as pltpu
from jax.sharding import PartitionSpec as P

D = 128
CAP = 2
THETA = 500000.0
SCALE = 1.0 / math.sqrt(D)
MESH = pl.DeviceIdType.MESH
F32 = jnp.float32
BF16 = jnp.bfloat16


def tables(count):
    half = D // 2
    inv = np.float32(THETA) ** (np.float32(-2.0) * np.arange(half, dtype=np.float32) / np.float32(D))
    angles = np.arange(count, dtype=np.float32)[:, None] * inv.astype(np.float32)[None, :]
    cos, sin = np.cos(angles), np.sin(angles)
    return np.concatenate([cos, cos, -sin, sin], axis=1).astype(np.float32)


def turn(x, table, sign):
    cos, sin = table[:, :D], table[:, D:]
    return x * cos + sign * (pltpu.roll(x, D // 2, 1) * sin)


def dot_nt(a, b):
    return lax.dot_general(a, b, (((1,), (1,)), ((), ())), preferred_element_type=F32)


def dot_nn(a, b):
    return lax.dot_general(a, b, (((1,), (0,)), ((), ())), preferred_element_type=F32)


def dot_tn(a, b):
    return lax.dot_general(a, b, (((0,), (0,)), ((), ())), preferred_element_type=F32)


def kernel(
    n, cites, lens_hbm, q_hbm, ok_hbm, ov_hbm, go_hbm, pk_hbm, pv_hbm, tab_hbm,
    gq, gok, gov, gpk, gpv,
    q, ok, ov, go, pk, pv, tab,
    lens, cites_in, sendbuf, fwd_in, backbuf, back_in,
    stage, gstage, qr, gl, ko, kp, dsp, es, dps, stats, wrow, slot_of, cite_of, place_of, bstage,
    low_sem, high_sem, load_sem, cs_sem, cr_sem, fs_sem, fr_sem, bs_sem, br_sem,
):
    rows = q.shape[0]
    heads = ok.shape[1] // D
    group = q.shape[1] // ok.shape[1]
    held, plen = pk.shape[0], pk.shape[1]
    ncite = cites.shape[2]
    prefix = ncite * plen
    me = lax.axis_index("enc")

    loads = [
        pltpu.make_async_copy(src, dst, load_sem.at[i])
        for i, (src, dst) in enumerate(
            [
                (pk_hbm.at[0], pk), (pv_hbm.at[0], pv), (tab_hbm, tab),
                (ok_hbm.at[0, 0], ok), (ov_hbm.at[0, 0], ov),
                (q_hbm.at[0, 0], q), (go_hbm.at[0, 0], go), (lens_hbm, lens),
            ]
        )
    ]
    barrier = pltpu.get_barrier_semaphore()

    def tell(sem, neighbour):
        pl.semaphore_signal(sem, inc=1, device_id={"enc": neighbour}, device_id_type=MESH)

    pl.when(me > 0)(lambda: tell(barrier, me - 1))
    pl.when(me < n - 1)(lambda: tell(barrier, me + 1))

    for load in loads:
        load.start()

    def ask(k):
        return pltpu.make_async_remote_copy(
            src_ref=cites.at[0], dst_ref=cites_in.at[k],
            send_sem=cs_sem.at[k], recv_sem=cr_sem.at[k],
            device_id={"enc": lax.rem(me + k, n)}, device_id_type=MESH,
        )

    def forward(k, h):
        return pltpu.make_async_remote_copy(
            src_ref=sendbuf.at[k, h], dst_ref=fwd_in.at[k, h],
            send_sem=fs_sem.at[k, h], recv_sem=fr_sem.at[k, h],
            device_id={"enc": lax.rem(me - k + n, n)}, device_id_type=MESH,
        )

    def back(k, h):
        return pltpu.make_async_remote_copy(
            src_ref=backbuf.at[k, h], dst_ref=back_in.at[k, h],
            send_sem=bs_sem.at[k, h], recv_sem=br_sem.at[k, h],
            device_id={"enc": lax.rem(me + k, n)}, device_id_type=MESH,
        )

    def unpack(source, target, h):
        @pl.loop(0, n, unroll=min(n, 4))
        def _(k):
            block = source[k, h].astype(F32)
            for r in range(CAP):
                target[k * CAP + r, 0] = block[r * plen : (r + 1) * plen]
                target[k * CAP + r, 1] = block[(CAP + r) * plen : (CAP + r + 1) * plen]

    def pick(k, target):
        low, high = held, -1
        for j in range(ncite):
            asked = cites[0, 0, j] if isinstance(k, int) and k == 0 else cites_in[k, 0, j]
            own = asked - me * held
            inside = (own >= 0) & (own < held)
            low = jnp.minimum(low, jnp.where(inside, own, held))
            high = jnp.maximum(high, jnp.where(inside, own, -1))
        wrow[k, 0] = low
        wrow[k, 1] = jnp.where(high > low, high, held)
        a = jnp.clip(low, 0, held - 1)
        b = jnp.clip(high, 0, held - 1)
        block = jnp.concatenate(
            [pk[a].astype(F32), pk[b].astype(F32), pv[a].astype(F32), pv[b].astype(F32)], axis=0
        ).astype(BF16)
        for h in range(heads):
            target[k, h] = block[:, h * D : (h + 1) * D]

    @pl.loop(0, ncite)
    def _(j):
        mine = cites[0, 0, j]
        owner = lax.div(mine, held)

        def count(i, total):
            other = cites[0, 0, i]
            return total + jnp.where((lax.div(other, held) == owner) & (other < mine), 1, 0)

        rank = lax.fori_loop(0, ncite, count, jnp.int32(0))
        slot_of[j] = lax.rem(owner - me + n, n) * CAP + rank

    @pl.loop(0, n * CAP)
    def _(s):
        def find(j, found):
            return jnp.where(slot_of[j] == s, j, found)

        cite_of[s] = lax.fori_loop(0, ncite, find, jnp.int32(ncite))

    loads[0].wait()
    loads[1].wait()
    pick(0, fwd_in)
    def serve(k):
        ask(k).wait_recv()
        pick(k, sendbuf)
        for h in range(2):
            forward(k, h).start()

    def reach(d):
        below, above = me >= d, me + d < n

        @pl.when(d > 1)
        def _():
            pl.when(below)(lambda: pl.semaphore_wait(low_sem.at[d], 1))
            pl.when(above)(lambda: pl.semaphore_wait(high_sem.at[d], 1))

        pl.when(below & (me < n - 1))(lambda: tell(low_sem.at[d + 1], me + 1))
        pl.when(above & (me > 0))(lambda: tell(high_sem.at[d + 1], me - 1))
        pl.when(below)(lambda: ask(n - d).start())
        pl.when(above)(lambda: ask(d).start())

    def serve_at(d):
        pl.when(me >= d)(lambda: serve(d))
        pl.when(me + d < n)(lambda: serve(n - d))

    pl.semaphore_wait(barrier, jnp.where(me > 0, 1, 0) + jnp.where(me < n - 1, 1, 0))
    reach(jnp.int32(1))

    @pl.loop(2, n)
    def _(d):
        reach(d)
        serve_at(d - 1)

    serve_at(n - 1)

    @pl.loop(2, heads)
    def _(h):
        @pl.loop(1, n)
        def _(d):
            pl.when(me >= d)(lambda: forward(d, h).start())
            pl.when(me + d < n)(lambda: forward(n - d, h).start())

    for load in loads[2:]:
        load.wait()

    limit = lens[0, 0, 0]
    live = lax.broadcasted_iota(jnp.int32, (rows, D), 0) < limit
    causal = lax.broadcasted_iota(jnp.int32, (rows, rows), 0) <= lax.broadcasted_iota(
        jnp.int32, (rows, rows), 1
    )

    def own(h):
        own_table = tab[prefix:, :]
        kcols = pl.ds(pl.multiple_of(h * D, D), D)
        key_own = turn(ok[:, kcols].astype(F32), own_table, 1.0).astype(BF16)
        ko[h] = key_own
        value_own = ov[:, kcols]
        for j in range(group):
            cols = pl.ds(pl.multiple_of((h * group + j) * D, D), D)
            query = turn(q[:, cols].astype(F32), own_table, 1.0).astype(BF16)
            grad = jnp.where(live, go[:, cols].astype(F32), 0.0).astype(BF16)
            qr[h, j] = query
            gl[h, j] = grad
            scores = jnp.where(causal, dot_nt(key_own, query) * SCALE, -1e30)
            top = jnp.max(scores, axis=0, keepdims=True)
            weights = jnp.exp(scores - top)
            gw = dot_nt(value_own, grad)
            es[h, j] = weights
            dps[h, j] = gw
            stats[h, j, 0:1, :] = top
            stats[h, j, 1:2, :] = jnp.sum(weights, axis=0, keepdims=True)
            stats[h, j, 2:3, :] = jnp.sum(weights * gw, axis=0, keepdims=True)

    @pl.loop(0, heads)
    def _(h):
        own(h)

    @pl.loop(0, held)
    def _(i):
        @pl.loop(0, n)
        def _(k):
            second = jnp.where(wrow[k, 1] == i, k * CAP + 1, n * CAP)
            place_of[i, k] = jnp.where(wrow[k, 0] == i, k * CAP, second)

    @pl.loop(1, n)
    def _(k):
        ask(k).wait_send()

    gstage[ncite] = jnp.zeros(gstage.shape[1:], F32)

    @pl.loop(0, heads)
    def _(h):
        @pl.loop(1, n)
        def _(k):
            forward(k, h).wait()

        unpack(fwd_in, stage, h)
        keys = jnp.concatenate([stage[slot_of[j], 0] for j in range(ncite)], axis=0)
        key_pas = turn(keys, tab[:prefix, :], 1.0).astype(BF16)
        kp[h] = key_pas
        value_pas = jnp.concatenate(
            [stage[slot_of[j], 1] for j in range(ncite)], axis=0
        ).astype(BF16)
        sum_keys = jnp.zeros((prefix, D), F32)
        sum_values = jnp.zeros((prefix, D), F32)
        for j in range(group):
            query, grad = qr[h, j], gl[h, j]
            top = stats[h, j, 0:1, :]
            scores = dot_nt(key_pas, query) * SCALE
            highest = jnp.maximum(top, jnp.max(scores, axis=0, keepdims=True))
            weights = jnp.exp(scores - highest)
            alpha = jnp.exp(top - highest)
            total = stats[h, j, 1:2, :] * alpha + jnp.sum(weights, axis=0, keepdims=True)
            inverse = 1.0 / total
            gw = dot_nt(value_pas, grad)
            center = (
                stats[h, j, 2:3, :] * alpha + jnp.sum(weights * gw, axis=0, keepdims=True)
            ) * inverse
            weights = weights * inverse
            grad_scores = (weights * (gw - center) * SCALE).astype(BF16)
            dsp[h, j] = grad_scores
            sum_values += dot_nn(weights.astype(BF16), grad)
            sum_keys += dot_nn(grad_scores, query)
            stats[h, j, 3:4, :] = alpha * inverse
            stats[h, j, 4:5, :] = center
        sum_keys = turn(sum_keys, tab[:prefix, :], -1.0)
        for j in range(ncite):
            gstage[j, 0] = sum_keys[j * plen : (j + 1) * plen]
            gstage[j, 1] = sum_values[j * plen : (j + 1) * plen]

        def give(k, target):
            a, b = cite_of[k * CAP], cite_of[k * CAP + 1]
            target[k, h] = jnp.concatenate(
                [gstage[a, 0], gstage[b, 0], gstage[a, 1], gstage[b, 1]], axis=0
            ).astype(BF16)

        @pl.loop(1, n)
        def _(k):
            give(k, backbuf)
            back(k, h).start()

        give(0, back_in)

    @pl.loop(0, heads)
    def _(h):
        key_pas = kp[h]
        kcols = pl.ds(pl.multiple_of(h * D, D), D)
        key_own = ko[h]
        own_table = tab[prefix:, :]
        own_keys = jnp.zeros((rows, D), F32)
        own_values = jnp.zeros((rows, D), F32)
        for j in range(group):
            query, grad = qr[h, j], gl[h, j]
            weights = es[h, j] * stats[h, j, 3:4, :]
            grad_scores = (weights * (dps[h, j] - stats[h, j, 4:5, :]) * SCALE).astype(BF16)
            own_values += dot_nn(weights.astype(BF16), grad)
            own_keys += dot_nn(grad_scores, query)
            grad_query = dot_tn(dsp[h, j], key_pas) + dot_tn(grad_scores, key_own)
            cols = pl.ds(pl.multiple_of((h * group + j) * D, D), D)
            gq[0, 0, :, cols] = turn(grad_query, own_table, -1.0).astype(BF16)
        gok[0, 0, :, kcols] = turn(own_keys, own_table, -1.0).astype(BF16)
        gov[0, 0, :, kcols] = own_values.astype(BF16)

    bstage[n * CAP] = jnp.zeros(bstage.shape[1:], F32)

    @pl.loop(0, heads)
    def _(h):
        @pl.loop(1, n)
        def _(k):
            back(k, h).wait_recv()
            back(k, h).wait_send()

        unpack(back_in, bstage, h)
        kcols = pl.ds(pl.multiple_of(h * D, D), D)
        for i in range(held):
            total = bstage[place_of[i, 0]]
            for k in range(1, n):
                total += bstage[place_of[i, k]]
            gpk[0, i, :, kcols] = total[0].astype(BF16)
            gpv[0, i, :, kcols] = total[1].astype(BF16)


def place(*refs):
    sems = refs[10]
    copies = [pltpu.make_async_copy(refs[i], refs[5 + i], sems.at[i]) for i in range(5)]
    for copy in copies:
        copy.start()
    for copy in copies:
        copy.wait()


def shards(n, queries, own_keys, own_values, grad_out, pkeys, pvalues, citations, lengths):
    rows, features = queries.shape[2:]
    kfeatures = own_keys.shape[3]
    heads, group = kfeatures // D, features // kfeatures
    held, plen = pkeys.shape[1], pkeys.shape[2]
    ncite = citations.shape[2]
    prefix = ncite * plen
    keys = prefix + rows
    slab = (n, heads, 2 * CAP * plen, D)
    table = jnp.asarray(tables(keys))
    hbm = pl.BlockSpec(memory_space=pltpu.HBM)
    smem = pl.BlockSpec(memory_space=pltpu.SMEM)
    vmem = pl.BlockSpec(memory_space=pltpu.VMEM)
    like = lambda x: jax.ShapeDtypeStruct(x.shape, x.dtype)
    flops = 2 * 5 * heads * group * rows * keys * D
    results = pl.pallas_call(
        functools.partial(kernel, n),
        out_shape=tuple(
            pltpu.VMEM(x.shape, x.dtype) for x in (queries, own_keys, own_values, pkeys, pvalues)
        ),
        in_specs=[smem] + [hbm] * 8,
        out_specs=(vmem,) * 5,
        scratch_shapes=[
            pltpu.VMEM((rows, features), BF16),
            pltpu.VMEM((rows, kfeatures), BF16),
            pltpu.VMEM((rows, kfeatures), BF16),
            pltpu.VMEM((rows, features), BF16),
            pltpu.VMEM((held, plen, kfeatures), BF16),
            pltpu.VMEM((held, plen, kfeatures), BF16),
            pltpu.VMEM((keys, 2 * D), F32),
            pltpu.SMEM((1, 1, 1), jnp.int32),
            pltpu.SMEM((n, 1, ncite), jnp.int32),
            pltpu.VMEM(slab, BF16),
            pltpu.VMEM(slab, BF16),
            pltpu.VMEM(slab, BF16),
            pltpu.VMEM(slab, BF16),
            pltpu.VMEM((n * CAP, 2, plen, D), F32),
            pltpu.VMEM((ncite + 1, 2, plen, D), F32),
            pltpu.VMEM((heads, group, rows, D), BF16),
            pltpu.VMEM((heads, group, rows, D), BF16),
            pltpu.VMEM((heads, rows, D), BF16),
            pltpu.VMEM((heads, prefix, D), BF16),
            pltpu.VMEM((heads, group, prefix, rows), BF16),
            pltpu.VMEM((heads, group, rows, rows), F32),
            pltpu.VMEM((heads, group, rows, rows), F32),
            pltpu.VMEM((heads, group, 8, rows), F32),
            pltpu.SMEM((n, CAP), jnp.int32),
            pltpu.SMEM((ncite,), jnp.int32),
            pltpu.SMEM((n * CAP,), jnp.int32),
            pltpu.SMEM((held, n), jnp.int32),
            pltpu.VMEM((n * CAP + 1, 2, plen, D), F32),
            pltpu.SemaphoreType.REGULAR((n + 1,)),
            pltpu.SemaphoreType.REGULAR((n + 1,)),
            pltpu.SemaphoreType.DMA((8,)),
            pltpu.SemaphoreType.DMA((n,)),
            pltpu.SemaphoreType.DMA((n,)),
            pltpu.SemaphoreType.DMA((n, heads)),
            pltpu.SemaphoreType.DMA((n, heads)),
            pltpu.SemaphoreType.DMA((n, heads)),
            pltpu.SemaphoreType.DMA((n, heads)),
        ],
        compiler_params=pltpu.CompilerParams(
            collective_id=0, has_side_effects=True, vmem_limit_bytes=61 * 1024 * 1024
        ),
        cost_estimate=pl.CostEstimate(
            flops=flops, bytes_accessed=6 * 1024 * 1024, transcendentals=heads * group * rows * keys
        ),
    )(citations, lengths[None], queries, own_keys, own_values, grad_out, pkeys, pvalues, table)
    return pl.pallas_call(
        place,
        out_shape=tuple(like(x) for x in (queries, own_keys, own_values, pkeys, pvalues)),
        in_specs=[pl.BlockSpec(memory_space=pl.ANY)] * 5,
        out_specs=(hbm,) * 5,
        scratch_shapes=[pltpu.SemaphoreType.DMA((5,))],
        compiler_params=pltpu.CompilerParams(vmem_limit_bytes=1024 * 1024),
        cost_estimate=pl.CostEstimate(flops=0, bytes_accessed=2 * 1024 * 1024, transcendentals=0),
    )(*results)


def solution(mesh):
    rows = P(("rep", "ans"), "enc", None, "sub")
    return jax.shard_map(
        functools.partial(shards, mesh.shape["enc"]),
        mesh=mesh,
        in_specs=(rows,) * 6 + (P(("rep", "ans"), "enc", None), P(("rep", "ans"), "enc")),
        out_specs=(rows,) * 5,
        check_vma=False,
    )
```

```python
import functools
import math

import jax
import jax.numpy as jnp
import numpy as np
from jax import lax
from jax.experimental import pallas as pl
from jax.experimental.pallas import tpu as pltpu
from jax.sharding import PartitionSpec as P

D = 128
CAP = 2
THETA = 500000.0
SCALE = 1.0 / math.sqrt(D)
MESH = pl.DeviceIdType.MESH
F32 = jnp.float32
BF16 = jnp.bfloat16


def tables(count):
    half = D // 2
    inv = np.float32(THETA) ** (np.float32(-2.0) * np.arange(half, dtype=np.float32) / np.float32(D))
    angles = np.arange(count, dtype=np.float32)[:, None] * inv.astype(np.float32)[None, :]
    cos, sin = np.cos(angles), np.sin(angles)
    return np.concatenate([cos, cos, -sin, sin], axis=1).astype(np.float32)


def turn(x, table, sign):
    cos, sin = table[:, :D], table[:, D:]
    return x * cos + sign * (pltpu.roll(x, D // 2, 1) * sin)


def dot_nt(a, b):
    return lax.dot_general(a, b, (((1,), (1,)), ((), ())), preferred_element_type=F32)


def dot_nn(a, b):
    return lax.dot_general(a, b, (((1,), (0,)), ((), ())), preferred_element_type=F32)


def dot_tn(a, b):
    return lax.dot_general(a, b, (((0,), (0,)), ((), ())), preferred_element_type=F32)


def kernel(
    n, cites, lens_hbm, q_hbm, ok_hbm, ov_hbm, go_hbm, pk_hbm, pv_hbm, tab_hbm,
    gq, gok, gov, gpk, gpv,
    q, ok, ov, go, pk, pv, tab,
    lens, cites_in, sendbuf, fwd_in, backbuf, back_in,
    stage, gstage, qr, gl, ko, kp, dsp, es, dps, stats, wrow, slot_of, cite_of, place_of, bstage,
    low_sem, high_sem, load_sem, cs_sem, cr_sem, fs_sem, fr_sem, bs_sem, br_sem,
):
    rows = q.shape[0]
    heads = ok.shape[1] // D
    group = q.shape[1] // ok.shape[1]
    held, plen = pk.shape[0], pk.shape[1]
    ncite = cites.shape[2]
    prefix = ncite * plen
    me = lax.axis_index("enc")

    loads = [
        pltpu.make_async_copy(src, dst, load_sem.at[i])
        for i, (src, dst) in enumerate(
            [
                (pk_hbm.at[0], pk), (pv_hbm.at[0], pv), (tab_hbm, tab),
                (ok_hbm.at[0, 0], ok), (ov_hbm.at[0, 0], ov),
                (q_hbm.at[0, 0], q), (go_hbm.at[0, 0], go), (lens_hbm, lens),
            ]
        )
    ]
    barrier = pltpu.get_barrier_semaphore()

    def tell(sem, neighbour):
        pl.semaphore_signal(sem, inc=1, device_id={"enc": neighbour}, device_id_type=MESH)

    pl.when(me > 0)(lambda: tell(barrier, me - 1))
    pl.when(me < n - 1)(lambda: tell(barrier, me + 1))

    for load in loads:
        load.start()

    def ask(k):
        return pltpu.make_async_remote_copy(
            src_ref=cites.at[0], dst_ref=cites_in.at[k],
            send_sem=cs_sem.at[k], recv_sem=cr_sem.at[k],
            device_id={"enc": lax.rem(me + k, n)}, device_id_type=MESH,
        )

    def forward(k, h):
        return pltpu.make_async_remote_copy(
            src_ref=sendbuf.at[k, h], dst_ref=fwd_in.at[k, h],
            send_sem=fs_sem.at[k, h], recv_sem=fr_sem.at[k, h],
            device_id={"enc": lax.rem(me - k + n, n)}, device_id_type=MESH,
        )

    def back(k, h):
        return pltpu.make_async_remote_copy(
            src_ref=backbuf.at[k, h], dst_ref=back_in.at[k, h],
            send_sem=bs_sem.at[k, h], recv_sem=br_sem.at[k, h],
            device_id={"enc": lax.rem(me + k, n)}, device_id_type=MESH,
        )

    def unpack(source, target, h):
        @pl.loop(0, n, unroll=min(n, 4))
        def _(k):
            block = source[k, h].astype(F32)
            for r in range(CAP):
                target[k * CAP + r, 0] = block[r * plen : (r + 1) * plen]
                target[k * CAP + r, 1] = block[(CAP + r) * plen : (CAP + r + 1) * plen]

    def pick(k, target):
        low, high = held, -1
        for j in range(ncite):
            asked = cites[0, 0, j] if isinstance(k, int) and k == 0 else cites_in[k, 0, j]
            own = asked - me * held
            inside = (own >= 0) & (own < held)
            low = jnp.minimum(low, jnp.where(inside, own, held))
            high = jnp.maximum(high, jnp.where(inside, own, -1))
        wrow[k, 0] = low
        wrow[k, 1] = jnp.where(high > low, high, held)
        a = jnp.clip(low, 0, held - 1)
        b = jnp.clip(high, 0, held - 1)
        block = jnp.concatenate(
            [pk[a].astype(F32), pk[b].astype(F32), pv[a].astype(F32), pv[b].astype(F32)], axis=0
        ).astype(BF16)
        for h in range(heads):
            target[k, h] = block[:, h * D : (h + 1) * D]

    @pl.loop(0, ncite)
    def _(j):
        mine = cites[0, 0, j]
        owner = lax.div(mine, held)

        def count(i, total):
            other = cites[0, 0, i]
            return total + jnp.where((lax.div(other, held) == owner) & (other < mine), 1, 0)

        rank = lax.fori_loop(0, ncite, count, jnp.int32(0))
        slot_of[j] = lax.rem(owner - me + n, n) * CAP + rank

    @pl.loop(0, n * CAP)
    def _(s):
        def find(j, found):
            return jnp.where(slot_of[j] == s, j, found)

        cite_of[s] = lax.fori_loop(0, ncite, find, jnp.int32(ncite))

    loads[0].wait()
    loads[1].wait()
    pick(0, fwd_in)
    def serve(k):
        ask(k).wait_recv()
        pick(k, sendbuf)
        for h in range(2):
            forward(k, h).start()

    def reach(d):
        below, above = me >= d, me + d < n

        @pl.when(d > 1)
        def _():
            pl.when(below)(lambda: pl.semaphore_wait(low_sem.at[d], 1))
            pl.when(above)(lambda: pl.semaphore_wait(high_sem.at[d], 1))

        pl.when(below & (me < n - 1))(lambda: tell(low_sem.at[d + 1], me + 1))
        pl.when(above & (me > 0))(lambda: tell(high_sem.at[d + 1], me - 1))
        pl.when(below)(lambda: ask(n - d).start())
        pl.when(above)(lambda: ask(d).start())

    def serve_at(d):
        pl.when(me >= d)(lambda: serve(d))
        pl.when(me + d < n)(lambda: serve(n - d))

    pl.semaphore_wait(barrier, jnp.where(me > 0, 1, 0) + jnp.where(me < n - 1, 1, 0))
    reach(jnp.int32(1))

    @pl.loop(2, n)
    def _(d):
        reach(d)
        serve_at(d - 1)

    serve_at(n - 1)

    @pl.loop(2, heads)
    def _(h):
        @pl.loop(1, n)
        def _(d):
            pl.when(me >= n - d)(lambda: forward(n - d, h).start())
            pl.when(me + n - d < n)(lambda: forward(d, h).start())

    for load in loads[2:]:
        load.wait()

    limit = lens[0, 0, 0]
    live = lax.broadcasted_iota(jnp.int32, (rows, D), 0) < limit
    causal = lax.broadcasted_iota(jnp.int32, (rows, rows), 0) <= lax.broadcasted_iota(
        jnp.int32, (rows, rows), 1
    )

    def own(h):
        own_table = tab[prefix:, :]
        kcols = pl.ds(pl.multiple_of(h * D, D), D)
        key_own = turn(ok[:, kcols].astype(F32), own_table, 1.0).astype(BF16)
        ko[h] = key_own
        value_own = ov[:, kcols]
        for j in range(group):
            cols = pl.ds(pl.multiple_of((h * group + j) * D, D), D)
            query = turn(q[:, cols].astype(F32), own_table, 1.0).astype(BF16)
            grad = jnp.where(live, go[:, cols].astype(F32), 0.0).astype(BF16)
            qr[h, j] = query
            gl[h, j] = grad
            scores = jnp.where(causal, dot_nt(key_own, query) * SCALE, -1e30)
            top = jnp.max(scores, axis=0, keepdims=True)
            weights = jnp.exp(scores - top)
            gw = dot_nt(value_own, grad)
            es[h, j] = weights
            dps[h, j] = gw
            stats[h, j, 0:1, :] = top
            stats[h, j, 1:2, :] = jnp.sum(weights, axis=0, keepdims=True)
            stats[h, j, 2:3, :] = jnp.sum(weights * gw, axis=0, keepdims=True)

    @pl.loop(0, heads)
    def _(h):
        own(h)

    @pl.loop(0, held)
    def _(i):
        @pl.loop(0, n)
        def _(k):
            second = jnp.where(wrow[k, 1] == i, k * CAP + 1, n * CAP)
            place_of[i, k] = jnp.where(wrow[k, 0] == i, k * CAP, second)

    @pl.loop(1, n)
    def _(k):
        ask(k).wait_send()

    gstage[ncite] = jnp.zeros(gstage.shape[1:], F32)

    @pl.loop(0, heads)
    def _(h):
        @pl.loop(1, n)
        def _(k):
            forward(k, h).wait()

        unpack(fwd_in, stage, h)
        keys = jnp.concatenate([stage[slot_of[j], 0] for j in range(ncite)], axis=0)
        key_pas = turn(keys, tab[:prefix, :], 1.0).astype(BF16)
        kp[h] = key_pas
        value_pas = jnp.concatenate(
            [stage[slot_of[j], 1] for j in range(ncite)], axis=0
        ).astype(BF16)
        sum_keys = jnp.zeros((prefix, D), F32)
        sum_values = jnp.zeros((prefix, D), F32)
        for j in range(group):
            query, grad = qr[h, j], gl[h, j]
            top = stats[h, j, 0:1, :]
            scores = dot_nt(key_pas, query) * SCALE
            highest = jnp.maximum(top, jnp.max(scores, axis=0, keepdims=True))
            weights = jnp.exp(scores - highest)
            alpha = jnp.exp(top - highest)
            total = stats[h, j, 1:2, :] * alpha + jnp.sum(weights, axis=0, keepdims=True)
            inverse = 1.0 / total
            gw = dot_nt(value_pas, grad)
            center = (
                stats[h, j, 2:3, :] * alpha + jnp.sum(weights * gw, axis=0, keepdims=True)
            ) * inverse
            weights = weights * inverse
            grad_scores = (weights * (gw - center) * SCALE).astype(BF16)
            dsp[h, j] = grad_scores
            sum_values += dot_nn(weights.astype(BF16), grad)
            sum_keys += dot_nn(grad_scores, query)
            stats[h, j, 3:4, :] = alpha * inverse
            stats[h, j, 4:5, :] = center
        sum_keys = turn(sum_keys, tab[:prefix, :], -1.0)
        for j in range(ncite):
            gstage[j, 0] = sum_keys[j * plen : (j + 1) * plen]
            gstage[j, 1] = sum_values[j * plen : (j + 1) * plen]

        def give(k, target):
            a, b = cite_of[k * CAP], cite_of[k * CAP + 1]
            target[k, h] = jnp.concatenate(
                [gstage[a, 0], gstage[b, 0], gstage[a, 1], gstage[b, 1]], axis=0
            ).astype(BF16)

        def send(k):
            give(k, backbuf)
            back(k, h).start()

        @pl.loop(1, n)
        def _(d):
            pl.when(me + n - d < n)(lambda: send(n - d))
            pl.when(me >= n - d)(lambda: send(d))

        give(0, back_in)

    @pl.loop(0, heads)
    def _(h):
        key_pas = kp[h]
        kcols = pl.ds(pl.multiple_of(h * D, D), D)
        key_own = ko[h]
        own_table = tab[prefix:, :]
        own_keys = jnp.zeros((rows, D), F32)
        own_values = jnp.zeros((rows, D), F32)
        for j in range(group):
            query, grad = qr[h, j], gl[h, j]
            weights = es[h, j] * stats[h, j, 3:4, :]
            grad_scores = (weights * (dps[h, j] - stats[h, j, 4:5, :]) * SCALE).astype(BF16)
            own_values += dot_nn(weights.astype(BF16), grad)
            own_keys += dot_nn(grad_scores, query)
            grad_query = dot_tn(dsp[h, j], key_pas) + dot_tn(grad_scores, key_own)
            cols = pl.ds(pl.multiple_of((h * group + j) * D, D), D)
            gq[0, 0, :, cols] = turn(grad_query, own_table, -1.0).astype(BF16)
        gok[0, 0, :, kcols] = turn(own_keys, own_table, -1.0).astype(BF16)
        gov[0, 0, :, kcols] = own_values.astype(BF16)

    bstage[n * CAP] = jnp.zeros(bstage.shape[1:], F32)

    @pl.loop(0, heads)
    def _(h):
        @pl.loop(1, n)
        def _(k):
            back(k, h).wait_recv()
            back(k, h).wait_send()

        unpack(back_in, bstage, h)
        kcols = pl.ds(pl.multiple_of(h * D, D), D)
        for i in range(held):
            total = bstage[place_of[i, 0]]
            for k in range(1, n):
                total += bstage[place_of[i, k]]
            gpk[0, i, :, kcols] = total[0].astype(BF16)
            gpv[0, i, :, kcols] = total[1].astype(BF16)


def place(*refs):
    sems = refs[10]
    copies = [pltpu.make_async_copy(refs[i], refs[5 + i], sems.at[i]) for i in range(5)]
    for copy in copies:
        copy.start()
    for copy in copies:
        copy.wait()


def shards(n, queries, own_keys, own_values, grad_out, pkeys, pvalues, citations, lengths):
    rows, features = queries.shape[2:]
    kfeatures = own_keys.shape[3]
    heads, group = kfeatures // D, features // kfeatures
    held, plen = pkeys.shape[1], pkeys.shape[2]
    ncite = citations.shape[2]
    prefix = ncite * plen
    keys = prefix + rows
    slab = (n, heads, 2 * CAP * plen, D)
    table = jnp.asarray(tables(keys))
    hbm = pl.BlockSpec(memory_space=pltpu.HBM)
    smem = pl.BlockSpec(memory_space=pltpu.SMEM)
    vmem = pl.BlockSpec(memory_space=pltpu.VMEM)
    like = lambda x: jax.ShapeDtypeStruct(x.shape, x.dtype)
    flops = 2 * 5 * heads * group * rows * keys * D
    results = pl.pallas_call(
        functools.partial(kernel, n),
        out_shape=tuple(
            pltpu.VMEM(x.shape, x.dtype) for x in (queries, own_keys, own_values, pkeys, pvalues)
        ),
        in_specs=[smem] + [hbm] * 8,
        out_specs=(vmem,) * 5,
        scratch_shapes=[
            pltpu.VMEM((rows, features), BF16),
            pltpu.VMEM((rows, kfeatures), BF16),
            pltpu.VMEM((rows, kfeatures), BF16),
            pltpu.VMEM((rows, features), BF16),
            pltpu.VMEM((held, plen, kfeatures), BF16),
            pltpu.VMEM((held, plen, kfeatures), BF16),
            pltpu.VMEM((keys, 2 * D), F32),
            pltpu.SMEM((1, 1, 1), jnp.int32),
            pltpu.SMEM((n, 1, ncite), jnp.int32),
            pltpu.VMEM(slab, BF16),
            pltpu.VMEM(slab, BF16),
            pltpu.VMEM(slab, BF16),
            pltpu.VMEM(slab, BF16),
            pltpu.VMEM((n * CAP, 2, plen, D), F32),
            pltpu.VMEM((ncite + 1, 2, plen, D), F32),
            pltpu.VMEM((heads, group, rows, D), BF16),
            pltpu.VMEM((heads, group, rows, D), BF16),
            pltpu.VMEM((heads, rows, D), BF16),
            pltpu.VMEM((heads, prefix, D), BF16),
            pltpu.VMEM((heads, group, prefix, rows), BF16),
            pltpu.VMEM((heads, group, rows, rows), F32),
            pltpu.VMEM((heads, group, rows, rows), F32),
            pltpu.VMEM((heads, group, 8, rows), F32),
            pltpu.SMEM((n, CAP), jnp.int32),
            pltpu.SMEM((ncite,), jnp.int32),
            pltpu.SMEM((n * CAP,), jnp.int32),
            pltpu.SMEM((held, n), jnp.int32),
            pltpu.VMEM((n * CAP + 1, 2, plen, D), F32),
            pltpu.SemaphoreType.REGULAR((n + 1,)),
            pltpu.SemaphoreType.REGULAR((n + 1,)),
            pltpu.SemaphoreType.DMA((8,)),
            pltpu.SemaphoreType.DMA((n,)),
            pltpu.SemaphoreType.DMA((n,)),
            pltpu.SemaphoreType.DMA((n, heads)),
            pltpu.SemaphoreType.DMA((n, heads)),
            pltpu.SemaphoreType.DMA((n, heads)),
            pltpu.SemaphoreType.DMA((n, heads)),
        ],
        compiler_params=pltpu.CompilerParams(
            collective_id=0, has_side_effects=True, vmem_limit_bytes=61 * 1024 * 1024
        ),
        cost_estimate=pl.CostEstimate(
            flops=flops, bytes_accessed=6 * 1024 * 1024, transcendentals=heads * group * rows * keys
        ),
    )(citations, lengths[None], queries, own_keys, own_values, grad_out, pkeys, pvalues, table)
    return pl.pallas_call(
        place,
        out_shape=tuple(like(x) for x in (queries, own_keys, own_values, pkeys, pvalues)),
        in_specs=[pl.BlockSpec(memory_space=pl.ANY)] * 5,
        out_specs=(hbm,) * 5,
        scratch_shapes=[pltpu.SemaphoreType.DMA((5,))],
        compiler_params=pltpu.CompilerParams(vmem_limit_bytes=1024 * 1024),
        cost_estimate=pl.CostEstimate(flops=0, bytes_accessed=2 * 1024 * 1024, transcendentals=0),
    )(*results)


def solution(mesh):
    rows = P(("rep", "ans"), "enc", None, "sub")
    return jax.shard_map(
        functools.partial(shards, mesh.shape["enc"]),
        mesh=mesh,
        in_specs=(rows,) * 6 + (P(("rep", "ans"), "enc", None), P(("rep", "ans"), "enc")),
        out_specs=(rows,) * 5,
        check_vma=False,
    )
```
